32 devices in a mesh: front: 2 (over core), grid: 4 (over y, x), depth: 4 (over z).
Axes of the slice: x: 2, y: 2, z: 4, core: 2. Of those that a mesh axis runs over, the one named last changes fastest.
Arguments:
- panel_base: float32 [2, 4, 4, 256, 256], P('front', None, 'grid'), as said below
- slab_base: float32 [2, 4, 4, 256, 1024], P('front', None, 'grid', None, 'depth'), may hold values from -6 to 6
- child_tiles: float32 [2, 4, 4, 4, 256, 256], P('front', 'grid', 'depth'), may hold values from -3 to 3
- child_maps: int32 [2, 4, 4, 4, 2], P('front', 'grid', 'depth'), may hold values from 0 to 15, as said below
- front_orders: int32 [2], P('front'), may hold values from 1280 to 4096, as said below
Outputs:
- panel_factor: float32 [2, 4, 4, 256, 256], P('front', None, 'grid')
- schur: float32 [2, 4, 4, 256, 1024], P('front', None, 'grid', None, 'depth')
The draws below stay inside these ranges and needn't reach their ends.
Inputs may be any that keep to these rules, and one draw needn't show every extreme that they name: Rows r = 0, g = 0 of each front's panel_base form a symmetric positive definite tile. `child_maps`: entry 0 is a parent tile row, entry 1 a tile column from 0 to 4, never both 0. A tile's owner is its parent tile row modulo 4; among one device's 4 tiles at most 2 have the same owner, and in every front one owner receives exactly 2 tiles from every device. `front_orders`: A multiple of 256; in every draw some front has the order 4096.
All inputs are finite; a program needn't handle non-finite values.
Results may differ from the reference program's by a relative error of at most 0.0003.
Values sent between devices are 32-bit elements; how exact they have to be, the bound alone decides.
A program may use at most 64 MiB of HBM per device.

```python
import jax
import jax.numpy as jnp
from jax import lax

TILE = 256
ORDER = 4096
NEXT = 4
CAP = 2
KIDS = 4
ROUNDS = 4
SLAB = 1024
FRONTS = 2
N_GRID = 4
N_DEPTH = 4


def draw_panel_base(key, part):
    key = jax.random.fold_in(key, 31)
    noise_key, diag_key = jax.random.split(key)
    shape = (FRONTS, ROUNDS, N_GRID, TILE, TILE)
    noise = jnp.clip(jax.random.normal(noise_key, shape, jnp.float32), -4.0, 4.0)
    corner = noise[:, 0, 0]
    symmetric = 0.5 * (corner + jnp.swapaxes(corner, -1, -2))
    diagonal = jax.random.uniform(diag_key, (FRONTS, TILE), jnp.float32, 2.0, 4.0) * TILE ** 0.5
    corner = symmetric + jnp.eye(TILE, dtype=jnp.float32)[None] * diagonal[:, None, :]
    return noise.at[:, 0, 0].set(corner)


def draw_child_maps(key, part):
    key = jax.random.fold_in(key, 57)
    star_key, score_key, round_key, column_key = jax.random.split(key, 4)
    shape = (FRONTS, N_GRID, N_DEPTH, KIDS)
    star = jax.random.randint(star_key, (FRONTS, 1, 1, 1), 0, N_GRID)
    scores = jax.random.randint(score_key, (FRONTS, N_GRID, N_DEPTH, N_GRID - 1), 0, 65536) * N_GRID + jnp.arange(N_GRID - 1)
    order_perm = jnp.argsort(scores, axis=-1, stable=True).astype(jnp.int32)
    others = (star + 1 + order_perm) % N_GRID
    pairs = jnp.concatenate([jnp.broadcast_to(star, (FRONTS, N_GRID, N_DEPTH, 1)), others[..., :KIDS // CAP - 1]], axis=-1)
    owners = jnp.repeat(pairs, CAP, axis=-1)
    rounds_drawn = jax.random.randint(round_key, shape, 0, ROUNDS)
    parent_row = owners + N_GRID * rounds_drawn
    parent_col = jax.random.randint(column_key, shape, 0, NEXT + 1)
    parent_col = jnp.where((parent_row == 0) & (parent_col == 0), 1, parent_col)
    return jnp.stack([parent_row, parent_col], axis=-1).astype(jnp.int32)


def draw_front_orders(key, part):
    key = jax.random.fold_in(key, 83)
    count_key, top_key = jax.random.split(key)
    counts = jax.random.randint(count_key, (FRONTS,), NEXT + 1, ORDER // TILE + 1)
    top = jax.random.randint(top_key, (), 0, FRONTS)
    counts = jnp.where(jnp.arange(FRONTS) == top, ORDER // TILE, counts)
    return (counts * TILE).astype(jnp.int32)


def steps_of(rng, extent, shards, low, top_value):
    gain = 1.0
    for position, parts in shards:
        draws = jax.random.uniform(jax.random.fold_in(jax.random.fold_in(rng, 6), position), (parts,), jnp.float32, low / len(shards), top_value / len(shards))
        gain = gain * jnp.repeat(jnp.exp(draws), extent[position] // parts).reshape((-1,) + (1,) * (len(extent) - 1 - position))
    return gain


def gaussian(own_key, dims, width, bound, cuts=(), kind=jnp.bfloat16):
    gain = steps_of(own_key, dims, cuts, -0.22, 0.18) if cuts else 1.0
    values = jax.random.normal(own_key, dims, jnp.float32) * width * gain
    return jnp.minimum(jnp.maximum(values, -bound), bound).astype(kind)


def setup_inputs(seed: int = 0) -> dict:
    key_list = jax.random.split(jax.random.key(seed), 6)
    return {
        "panel_base": draw_panel_base(jax.random.fold_in(key_list[5], 71), 0),
        "slab_base": gaussian(key_list[1], (FRONTS, ROUNDS, N_GRID, TILE, SLAB), 1.0, 6.0, ((0, 2), (2, 4), (4, 4)), jnp.float32),
        "child_tiles": gaussian(key_list[2], (FRONTS, N_GRID, N_DEPTH, KIDS, TILE, TILE), 0.5, 3.0, ((0, 2), (1, 4), (2, 4)), jnp.float32),
        "child_maps": draw_child_maps(jax.random.fold_in(key_list[5], 71), 0),
        "front_orders": draw_front_orders(jax.random.fold_in(key_list[5], 71), 0),
    }


def one_front(inputs):
    panel_tiles, slab_tiles, child_part, map_part, order_value = inputs
    tile_count = ORDER // TILE
    panel_flat = panel_tiles.reshape(tile_count, TILE, TILE)
    slab_flat = slab_tiles.reshape(tile_count, TILE, NEXT, TILE).transpose(0, 2, 1, 3)
    window = jnp.concatenate([panel_flat[:, None], slab_flat], axis=1)
    positions = (map_part[..., 0] * (NEXT + 1) + map_part[..., 1]).reshape(-1).astype(jnp.int32)
    added = jax.ops.segment_sum(child_part.reshape(-1, TILE, TILE), positions, num_segments=tile_count * (NEXT + 1))
    window = window + added.reshape(tile_count, NEXT + 1, TILE, TILE)
    live_rows = (jnp.arange(tile_count) * TILE < order_value).astype(jnp.float32)
    window = window * live_rows[:, None, None, None]
    corner_factor = jnp.linalg.cholesky(window[0, 0])
    solved = lax.linalg.triangular_solve(jnp.broadcast_to(corner_factor, (tile_count, TILE, TILE)), window[:, 0], left_side=False, lower=True, transpose_a=True)
    factored = jnp.concatenate([corner_factor[None], solved[1:]], axis=0)
    wanted = factored[1:NEXT + 1]
    update = jnp.einsum('tai,jbi->tjab', factored, wanted, precision=lax.Precision.HIGHEST)
    schur_block = window[:, 1:] - update
    schur_block = schur_block.transpose(0, 2, 1, 3).reshape(ROUNDS, N_GRID, TILE, SLAB)
    return (factored.reshape(ROUNDS, N_GRID, TILE, TILE), schur_block)

def reference(panel_base, slab_base, child_tiles, child_maps, front_orders):
    panel_factor, schur = lax.map(one_front, (panel_base, slab_base, child_tiles, child_maps, front_orders))
    return (panel_factor, schur)
```

```python
import functools

import jax
import jax.numpy as jnp
from jax import lax
from jax.experimental import pallas as pl
from jax.experimental.pallas import tpu as pltpu
from jax.sharding import PartitionSpec as P

CAP = 2
CHUNK = 32
BLOCK = 64
HI = lax.Precision.HIGHEST


def dot(a, b, ca, cb):
    return lax.dot_general(
        a, b, (((ca,), (cb,)), ((), ())), precision=HI, preferred_element_type=jnp.float32
    )


def factor_block(w, b):
    tile = w.shape[0]
    s = b * BLOCK
    base = s // 128 * 128
    d = w[s : s + BLOCK, base : base + 128]
    if s != base:
        d = pltpu.roll(d, 128 - BLOCK, 1)
    row = lax.broadcasted_iota(jnp.int32, (BLOCK, 128), 0)
    lane = lax.broadcasted_iota(jnp.int32, (BLOCK, 128), 1)
    aug = jnp.where(lane < BLOCK, d, jnp.where(lane - BLOCK == row, 1.0, 0.0))

    def step(j, aug):
        at_row = jnp.where(row == j, aug, 0.0)
        at_both = jnp.where(lane == j, at_row, 0.0)
        col = jnp.sum(jnp.where(lane == j, aug, 0.0), axis=1, keepdims=True)
        pivot_row = jnp.sum(at_row, axis=0, keepdims=True)
        pivot = jnp.sum(jnp.sum(at_both, axis=0, keepdims=True), axis=1, keepdims=True)
        return jnp.where(row > j, aug - col * (pivot_row / pivot), aug)

    aug = lax.fori_loop(0, BLOCK, step, aug)
    diag = jnp.sum(jnp.where(lane == row, aug, 0.0), axis=1, keepdims=True)
    aug = aug / jnp.sqrt(diag)
    if s == base:
        inv = jnp.where(lane < BLOCK, pltpu.roll(aug, 128 - BLOCK, 1), 0.0)
    else:
        inv = jnp.where(lane >= BLOCK, aug, 0.0)
    rows = dot(inv, w[base : base + 128, :], 1, 0)
    w[s : s + BLOCK, :] = rows
    if s + BLOCK < tile:
        update = dot(rows[:, :tile], rows, 0, 0)
        w[s + BLOCK :, :] = w[s + BLOCK :, :] - update[s + BLOCK :, :]


def kernel(
    G, panel, slab, child, maps, orders, pout, sout,
    send, spos, recv, rpos, eslots, epos, cross_out, cross_in, mine, end_out, end_in,
    corner, fj, pf, w,
    corner_ss, corner_rs, pos_ss, pos_rs, a_ss, a_rs, ep_ss, ep_rs, e_ss, e_rs,
    c_ss, c_rs, t_ss, t_rs, f_ss, f_rs,
):
    R, tile, _ = panel.shape
    H = tile // CHUNK
    kids = child.shape[0]
    cols = 5
    g = lax.axis_index("grid")
    d = lax.axis_index("depth")
    is_mid = (d == 1) | (d == 2)
    is_end = (d == 0) | (d == 3)
    partner = d + 1 - 2 * (d % 2)
    other = 3 - d

    def peer(o):
        return (g + o) % G

    def copy(src, dst, ss, rs, axis, where):
        return pltpu.make_async_remote_copy(
            src_ref=src, dst_ref=dst, send_sem=ss, recv_sem=rs,
            device_id={axis: where}, device_id_type=pl.DeviceIdType.MESH,
        )

    barrier = pltpu.get_barrier_semaphore()
    for o in range(1, G):
        pl.semaphore_signal(barrier, inc=1, device_id={"grid": peer(o)}, device_id_type=pl.DeviceIdType.MESH)
    for o in range(1, 4):
        pl.semaphore_signal(barrier, inc=1, device_id={"depth": (d + o) % 4}, device_id_type=pl.DeviceIdType.MESH)
    pl.semaphore_wait(barrier, G - 1 + 3)

    def corner_copy(o):
        return copy(panel.at[0], corner, corner_ss.at[o], corner_rs, "grid", peer(o))

    @pl.when(g == 0)
    def _():
        for o in range(1, G):
            corner_copy(o).start()

    prow = [maps[k, 0] for k in range(kids)]
    pcol = [maps[k, 1] for k in range(kids)]
    owner = [x % G for x in prow]
    rank = []
    for k in range(kids):
        n = jnp.int32(0)
        for i in range(k):
            n = n + (owner[i] == owner[k]).astype(jnp.int32)
        rank.append(n)
    for o in [*range(1, G), 0]:
        to, to_pos = (recv, rpos) if o == 0 else (send, spos)
        for s in range(CAP):
            which, place = jnp.int32(0), jnp.int32(-1)
            for k in range(kids):
                hit = (owner[k] == peer(o)) & (rank[k] == s)
                which = jnp.where(hit, k, which)
                place = jnp.where(hit, prow[k] // G * cols + pcol[k], place)
            to_pos[CAP * o + s] = jnp.full((8, 128), place.astype(jnp.float32))

            def move(h, _):
                rows = pl.ds(pl.multiple_of(h * CHUNK, CHUNK), CHUNK)
                to[h, CAP * o + s] = child[which, rows, :]
                return 0

            lax.fori_loop(0, H, move, 0)

    def pos_copy(o):
        two = pl.ds(CAP * o, CAP)
        return copy(spos.at[two], rpos.at[two], pos_ss.at[o], pos_rs.at[o], "grid", peer(o))

    def a_copy(o, h):
        two = pl.ds(CAP * o, CAP)
        return copy(send.at[h, two], recv.at[h, two], a_ss.at[o, h], a_rs.at[o, h], "grid", peer(o))

    def epos_copy():
        return copy(rpos, epos, ep_ss, ep_rs, "depth", partner)

    def e_copy(h):
        return copy(recv.at[h], eslots.at[h], e_ss.at[h], e_rs.at[h], "depth", partner)

    def c_copy(h):
        return copy(cross_out.at[h], cross_in.at[h], c_ss.at[h], c_rs.at[h], "depth", other)

    def t_copy(h):
        return copy(end_out.at[h], end_in.at[h], t_ss.at[h], t_rs.at[h], "depth", partner)

    for o in range(1, G):
        pos_copy(o).start()
    for h in range(H):
        for o in range(1, G):
            a_copy(o, h).start()

    @pl.when(g == 0)
    def _():
        w[:, :tile] = panel[0]

    @pl.when(g != 0)
    def _():
        corner_copy(1).wait_recv()
        w[:, :tile] = corner[...]

    ii = lax.broadcasted_iota(jnp.int32, (tile, tile), 0)
    jj = lax.broadcasted_iota(jnp.int32, (tile, tile), 1)
    w[:, tile:] = jnp.where(ii == jj, 1.0, 0.0)

    for o in range(1, G):
        pos_copy(o).wait_recv()

    @pl.when(is_end)
    def _():
        epos_copy().start()

    @pl.when(is_mid)
    def _():
        epos_copy().wait_recv()

    def spread(h):
        far = [(r * cols + c).astype(jnp.float32) for c in (other + 1, 3 - partner + 1) for r in range(R)]
        near = [(r * cols + c).astype(jnp.float32) for c in (d + 1, partner + 1) for r in range(R)]
        mid = [jnp.float32(r * cols) for r in range(R)]
        wanted = far + near + mid

        def part(q, _):
            rows = pl.ds(pl.multiple_of(q * 8, 8), 8)
            for half in range(tile // 128):
                lanes = pl.ds(half * 128, 128)
                acc = [jnp.zeros((8, 128), jnp.float32) for _ in wanted]
                for data, pos in ((recv, rpos), (eslots, epos)):
                    for s in range(G * CAP):
                        x, where = data[h, s, rows, lanes], pos[s]
                        for p in range(len(wanted)):
                            acc[p] = acc[p] + jnp.where(where == wanted[p], x, 0.0)
                for p in range(2 * R):
                    cross_out[h, p, rows, lanes] = acc[p]
                    mine[h, p, rows, lanes] = acc[2 * R + p]
                for r in range(R):
                    cross_out[h, 2 * R + r, rows, lanes] = acc[4 * R + r]
                    mine[h, 2 * R + r, rows, lanes] = acc[4 * R + r]
            return 0

        lax.fori_loop(0, CHUNK // 8, part, 0)

    def stage_a(h):
        for o in range(1, G):
            a_copy(o, h).wait_recv()

        @pl.when(is_end)
        def _():
            e_copy(h).start()

        @pl.when(is_mid)
        def _():
            e_copy(h).wait_recv()
            spread(h)
            c_copy(h).start()

    row_j, owner_j = (d + 1) // G, (d + 1) % G

    def f_copy(o, h):
        rows = pl.ds(h * CHUNK, CHUNK)
        return copy(pf.at[row_j, rows], fj.at[rows], f_ss.at[o, h], f_rs.at[h], "grid", peer(o))

    def close(h, sums):
        rows = pl.ds(h * CHUNK, CHUNK)
        for r in range(R):
            slab_sum, panel_sum = sums(r)
            live = ((r * G + g) * tile < orders[0]).astype(jnp.float32)
            pf[r, rows, :] = (panel[r, rows, :] + panel_sum) * live
            sout[r, rows, :] = (slab[r, rows, :] + slab_sum) * live

        @pl.when(g == owner_j)
        def _():
            for o in range(1, G):
                f_copy(o, h).start()
            fj[rows, :] = pf[row_j, rows, :]

    def stage_b(h):
        @pl.when(is_mid)
        def _():
            c_copy(h).wait_recv()
            for r in range(R):
                end_out[h, r] = mine[h, R + r] + cross_in[h, R + r]
                end_out[h, R + r] = mine[h, 2 * R + r] + cross_in[h, 2 * R + r]
            t_copy(h).start()
            close(h, lambda r: (mine[h, r] + cross_in[h, r], end_out[h, R + r]))

    def stage_c(h):
        @pl.when(is_end)
        def _():
            t_copy(h).wait_recv()
            close(h, lambda r: (end_in[h, r], end_in[h, R + r]))

    blocks = tile // BLOCK
    per = H // blocks
    for b in range(blocks):
        for h in range(b * per, (b + 1) * per):
            stage_a(h)
        if b >= 1:
            for h in range((b - 1) * per, b * per):
                stage_b(h)
        factor_block(w, b)
    for h in range((blocks - 1) * per, H):
        stage_b(h)
    factor = jnp.where(ii >= jj, w[:, :tile].T, 0.0)
    inverse = jnp.where(ii >= jj, w[:, tile:], 0.0)
    for h in range(H):
        stage_c(h)

    for r in range(R):
        solved = dot(pf[r], inverse, 1, 1)
        if r == 0:
            solved = jnp.where(g == 0, factor, solved)
        pout[r] = solved

    @pl.when(g != owner_j)
    def _():
        for h in range(H):
            f_copy(1, h).wait_recv()

    wanted = dot(fj[...], inverse, 1, 1)
    for r in range(R):
        sout[r] = sout[r] - dot(pout[r], wanted, 1, 1)

    @pl.when(g == 0)
    def _():
        for o in range(1, G):
            corner_copy(o).wait_send()

    for o in range(1, G):
        pos_copy(o).wait_send()
        for h in range(H):
            a_copy(o, h).wait_send()

    @pl.when(is_end)
    def _():
        epos_copy().wait_send()
        for h in range(H):
            e_copy(h).wait_send()

    @pl.when(is_mid)
    def _():
        for h in range(H):
            c_copy(h).wait_send()
            t_copy(h).wait_send()

    @pl.when(g == owner_j)
    def _():
        for o in range(1, G):
            for h in range(H):
                f_copy(o, h).wait_send()


def on_device(G, panel_base, slab_base, child_tiles, child_maps, front_orders):
    R, tile = panel_base.shape[1], panel_base.shape[3]
    kids = child_tiles.shape[3]
    H = tile // CHUNK
    slots = G * CAP
    f32 = jnp.float32
    vm = lambda *shape: pltpu.VMEM(shape, f32)
    sem = lambda *shape: pltpu.SemaphoreType.DMA(shape)
    one = pltpu.SemaphoreType.DMA
    vmem = pl.BlockSpec(memory_space=pltpu.VMEM)
    smem = pl.BlockSpec(memory_space=pltpu.SMEM)
    pout, sout = pl.pallas_call(
        functools.partial(kernel, G),
        out_shape=[jax.ShapeDtypeStruct((R, tile, tile), f32)] * 2,
        in_specs=[vmem, vmem, vmem, smem, smem],
        out_specs=[vmem, vmem],
        scratch_shapes=[
            vm(H, slots, CHUNK, tile), vm(slots, 8, 128),
            vm(H, slots, CHUNK, tile), vm(slots, 8, 128),
            vm(H, slots, CHUNK, tile), vm(slots, 8, 128),
            vm(H, 3 * R, CHUNK, tile), vm(H, 3 * R, CHUNK, tile), vm(H, 3 * R, CHUNK, tile),
            vm(H, 2 * R, CHUNK, tile), vm(H, 2 * R, CHUNK, tile),
            vm(tile, tile), vm(tile, tile), vm(R, tile, tile), vm(tile, 2 * tile),
            sem(G), one, sem(G), sem(G), sem(G, H), sem(G, H), one, one, sem(H), sem(H),
            sem(H), sem(H), sem(H), sem(H), sem(G, H), sem(H),
        ],
        compiler_params=pltpu.CompilerParams(
            collective_id=0, has_side_effects=True, vmem_limit_bytes=50 * 1024 * 1024
        ),
    )(
        panel_base.reshape(R, tile, tile),
        slab_base.reshape(R, tile, tile),
        child_tiles.reshape(kids, tile, tile),
        child_maps.reshape(kids, 2),
        front_orders,
    )
    return pout.reshape(panel_base.shape), sout.reshape(slab_base.shape)


def solution(mesh):
    in_specs = (
        P("front", None, "grid", None, None),
        P("front", None, "grid", None, "depth"),
        P("front", "grid", "depth", None, None, None),
        P("front", "grid", "depth", None, None),
        P("front"),
    )
    out_specs = (P("front", None, "grid", None, None), P("front", None, "grid", None, "depth"))
    return jax.shard_map(
        functools.partial(on_device, mesh.shape["grid"]),
        mesh=mesh, in_specs=in_specs, out_specs=out_specs, check_vma=False,
    )
```
